32 devices in a mesh: mem: 8 (over z, x), pb: 4 (over y, core).
Axes of the slice: x: 2, y: 2, z: 4, core: 2. Of those that a mesh axis runs over, the one named last changes fastest.
Arguments:
- queries: bfloat16 [4096, 1024], P(('pb', 'mem')), may hold values from -9 to 9
- local_keys: bfloat16 [4096, 1024], P(('pb', 'mem')), may hold values from -9 to 9
- local_values: bfloat16 [4096, 1024], P(('pb', 'mem')), may hold values from -6 to 6
- memory_keys: bfloat16 [8192, 1024], P('mem'), may hold values from -11 to 11
- memory_values: bfloat16 [8192, 1024], P('mem'), may hold values from -6 to 6
- neighbour_index_rows: int32 [4096, 32], P(('pb', 'mem')), may hold values from 0 to 8191, as said below
- gate_bias: float32 [8], replicated, may hold values from -2.5 to 2.5
- out_weight: bfloat16 [1024, 1024], P('pb'), may hold values from -0.75 to 0.75
Outputs:
- layer_out: bfloat16 [4096, 1024], P(('pb', 'mem'))
The draws below stay inside these ranges and needn't reach their ends.
Inputs may be any that keep to these rules, and one draw needn't show every extreme that they name: `neighbour_index_rows`: memory shard o holds rows o * 1024 to (o + 1) * 1024 - 1. Among the 4096 ids of one device's rows, at most 1024 fall in any one shard, and exactly 1024 fall in some shard; for each index of pb, one shard receives exactly 1024 from every device with that index. Ids of a row may repeat.
All inputs are finite; a program needn't handle non-finite values.
Results may differ from the reference program's by a relative error of at most 0.01.
Values may be sent and summed in bfloat16 or wider, within the bound.
A program may use at most 192 MiB of HBM per device.

```python
import math
import jax
import jax.numpy as jnp
from jax import lax

D = 1024
H = 8
DH = 128
Q_DEV = 128
MEM_DEV = 1024
TOPK = 32
SHARDS = 8
TOKENS = 4096
MEMORY = 8192


def shared_fields(key):
    keys = jax.random.split(jax.random.fold_in(key, 5), 3)
    query_field = jnp.clip(jax.random.normal(keys[0], (TOKENS, D), jnp.float32), -6.0, 6.0)
    local_field = jnp.clip(jax.random.normal(keys[1], (TOKENS, D), jnp.float32), -6.0, 6.0)
    memory_field = jnp.clip(jax.random.normal(keys[2], (MEMORY, D), jnp.float32), -6.0, 6.0)
    shard_of = (jnp.arange(MEMORY) // MEM_DEV).astype(jnp.float32)
    ramp = 0.8 + 0.9 * shard_of / max(SHARDS - 1, 1)
    memory_field = memory_field * ramp[:, None]
    return (query_field, local_field, memory_field)


def draw_queries(key, part):
    return shared_fields(key)[0].astype(jnp.bfloat16)


def draw_local_keys(key, part):
    return shared_fields(key)[1].astype(jnp.bfloat16)


def draw_memory_keys(key, part):
    return shared_fields(key)[2].astype(jnp.bfloat16)


def draw_neighbour_index_rows(key, part):
    block_count = TOKENS // Q_DEV
    slot_count = Q_DEV * TOPK
    mean_load = slot_count // SHARDS
    pair_count = SHARDS // 2
    base_key = jax.random.fold_in(key, 11)

    def one_block(index):
        block_key = jax.random.fold_in(base_key, index)
        group_key = jax.random.fold_in(jax.random.fold_in(base_key, 100003), index // SHARDS)
        shard_order = jax.random.permutation(group_key, SHARDS)
        first_key, second_key, third_key = jax.random.split(block_key, 3)
        displacements = jax.random.randint(first_key, (pair_count,), 0, mean_load + 1)
        displacements = displacements.at[0].set(mean_load)
        paired = jnp.stack([mean_load + displacements, mean_load - displacements], 1).reshape(SHARDS).astype(jnp.int32)
        counts = jnp.zeros((SHARDS,), jnp.int32).at[shard_order].set(paired)
        bounds = jnp.cumsum(counts)
        slot_index = jnp.arange(slot_count, dtype=jnp.int32)
        sorted_owner = jnp.sum((slot_index[:, None] >= bounds[None, :]).astype(jnp.int32), axis=1)
        shuffle = jax.random.permutation(second_key, slot_count)
        owner = sorted_owner[shuffle]
        offset = jax.random.randint(third_key, (slot_count,), 0, MEM_DEV)
        return (owner * MEM_DEV + offset).reshape(Q_DEV, TOPK)
    result = jax.vmap(one_block)(jnp.arange(block_count, dtype=jnp.int32))
    return result.reshape(TOKENS, TOPK).astype(jnp.int32)


def steps_of(own_key, dims, shards, low, high):
    factor_of = 1.0
    for dim, blocks in shards:
        steps = jax.random.uniform(jax.random.fold_in(jax.random.fold_in(own_key, 6), dim), (blocks,), jnp.float32, low / len(shards), high / len(shards))
        factor_of = factor_of * jnp.repeat(jnp.exp(steps), dims[dim] // blocks).reshape((-1,) + (1,) * (len(dims) - 1 - dim))
    return factor_of


def noise(key, dims, width, bound, pieces=(), kind=jnp.bfloat16):
    level = steps_of(key, dims, pieces, -0.22, 0.18) if pieces else 1.0
    values = jax.random.normal(key, dims, jnp.float32) * width * level
    return jnp.minimum(jnp.maximum(values, -bound), bound).astype(kind)


def setup_inputs(seed: int = 0) -> dict:
    key_list = jax.random.split(jax.random.key(seed), 9)
    queries = draw_queries(jax.random.fold_in(key_list[8], 71), 0)
    local_keys = draw_local_keys(jax.random.fold_in(key_list[8], 71), 0)
    local_values = noise(key_list[2], (TOKENS, D), 1.0, 6.0, ((0, 32),))
    memory_keys = draw_memory_keys(jax.random.fold_in(key_list[8], 71), 0)
    memory_values = noise(key_list[4], (MEMORY, D), 1.0, 6.0, ((0, 8),))
    neighbour_index_rows = draw_neighbour_index_rows(jax.random.fold_in(key_list[8], 71), 0)
    gate_bias = jnp.clip(jax.random.uniform(key_list[6], (H,), jnp.float32, -2.5, 2.5), -2.5, 2.5)
    out_weight = noise(key_list[7], (D, D), (D // 16) ** -0.5, 0.75, ((0, 4),))
    return {"queries": queries, "local_keys": local_keys, "local_values": local_values, "memory_keys": memory_keys, "memory_values": memory_values, "neighbour_index_rows": neighbour_index_rows, "gate_bias": gate_bias, "out_weight": out_weight}


def reference(queries, local_keys, local_values, memory_keys, memory_values, neighbour_index_rows, gate_bias, out_weight):
    multiplier = DH ** -0.5
    segment_count = TOKENS // Q_DEV
    query_seg = queries.astype(jnp.float32).reshape(segment_count, Q_DEV, H, DH)
    key_seg = local_keys.astype(jnp.float32).reshape(segment_count, Q_DEV, H, DH)
    value_seg = local_values.astype(jnp.float32).reshape(segment_count, Q_DEV, H, DH)
    local_scores = jnp.einsum("sqhd,skhd->shqk", query_seg, key_seg) * multiplier
    causal = jnp.arange(Q_DEV)[:, None] >= jnp.arange(Q_DEV)[None, :]
    local_scores = jnp.where(causal[None, None], local_scores, -jnp.inf)
    local_peak = jnp.max(local_scores, axis=-1, keepdims=True)
    local_expo = jnp.exp(local_scores - local_peak)
    local_weights = (local_expo / jnp.sum(local_expo, axis=-1, keepdims=True)).astype(jnp.bfloat16)
    local_out = jnp.einsum("shqk,skhd->sqhd", local_weights.astype(jnp.float32), value_seg).reshape(TOKENS, H, DH)

    key_head_count = memory_keys.astype(jnp.float32).reshape(MEMORY, H, DH)
    value_heads = memory_values.astype(jnp.float32).reshape(MEMORY, H, DH)
    block = math.gcd(TOKENS, 256)

    def one_block(inputs):
        query_tile_block, id_block = inputs
        logit_scores = jnp.einsum("bvt,yvt->bvy", query_tile_block, key_head_count) * multiplier
        memory_peak = jnp.max(logit_scores, axis=2)
        memory_total = jnp.sum(jnp.exp(logit_scores - memory_peak[:, :, None]), axis=2)
        picked_keys = key_head_count[id_block]
        picked_scores = jnp.einsum("qhd,qthd->qth", query_tile_block, picked_keys) * multiplier
        retrieved = jnp.exp(picked_scores - memory_peak[:, None, :]).astype(jnp.bfloat16).astype(jnp.float32)
        numerator = jnp.einsum("qth,qthd->qhd", retrieved, value_heads[id_block])
        denominator = jnp.sum(retrieved, axis=1) + (TOPK / MEMORY) * memory_total
        return numerator / denominator[:, :, None]

    query_all = queries.astype(jnp.float32).reshape(TOKENS // block, block, H, DH)
    ids_all = neighbour_index_rows.reshape(TOKENS // block, block, TOPK).astype(jnp.int32)
    memory_out = lax.map(one_block, (query_all, ids_all)).reshape(TOKENS, H, DH)
    gate = jax.nn.sigmoid(gate_bias)[None, :, None]
    mixed = (gate * memory_out + (1.0 - gate) * local_out).reshape(TOKENS, D).astype(jnp.bfloat16)
    return jnp.dot(mixed, out_weight, preferred_element_type=jnp.float32).astype(jnp.bfloat16)
```

```python
import functools

import jax
import jax.numpy as jnp
from jax import lax
from jax.experimental import pallas as pl
from jax.experimental.pallas import tpu as pltpu
from jax.sharding import PartitionSpec as P

LOG2E = 1.4426950408889634
F32 = jnp.float32
BF16 = jnp.bfloat16


def dot(a, b):
    return jnp.dot(a, b, preferred_element_type=F32)


def dot_t(a, b):
    return lax.dot_general(a, b, (((1,), (1,)), ((), ())), preferred_element_type=F32)


def count_block(ids, rows, memory_rows, dtype):
    cols = lax.broadcasted_iota(jnp.int32, (rows, memory_rows), 1)
    total = jnp.zeros((rows, memory_rows), F32)
    for t in range(ids.shape[1]):
        total = total + jnp.where(ids[:, t : t + 1] == cols, 1.0, 0.0)
    return total.astype(dtype)


def shard_kernel(heads, scale, background, ids_ref, q_ref, k_ref, v_ref, n_ref, st_ref, kt_ref):
    memory_rows, width = k_ref.shape
    size = width // heads
    rows = q_ref.shape[0]

    @pl.when(pl.program_id(0) == 0)
    def _():
        for h in range(heads):
            hs = slice(h * size, (h + 1) * size)
            kt_ref[hs, :] = k_ref[:, hs].T

    count = count_block(ids_ref[...], rows, memory_rows, F32)
    lane = lax.broadcasted_iota(jnp.int32, (rows, 128), 1)
    stats = jnp.zeros((rows, 128), F32)
    for h in range(heads):
        hs = slice(h * size, (h + 1) * size)
        s = dot(q_ref[:, hs], kt_ref[hs, :])
        peak = jnp.max(s, axis=1, keepdims=True)
        e = jnp.exp2((s - peak) * (scale * LOG2E))
        w = e * count
        total = jnp.sum(e, axis=1, keepdims=True)
        den = jnp.sum(w, axis=1, keepdims=True)
        n_ref[:, hs] = dot(w.astype(BF16), v_ref[:, hs]).astype(BF16)
        stats = jnp.where(lane == h, peak * scale, stats)
        stats = jnp.where(lane == heads + h, den + background * total, stats)
    st_ref[...] = stats


def final_kernel(heads, scale, q_ref, lk_ref, lv_ref, n_ref, st_ref, gate_ref, ow_ref, out_ref, mixed):
    shards, rows, width = n_ref.shape
    size = width // heads
    causal = lax.broadcasted_iota(jnp.int32, (rows, rows), 0) >= lax.broadcasted_iota(
        jnp.int32, (rows, rows), 1
    )
    for h in range(heads):
        hs = slice(h * size, (h + 1) * size)
        s = dot_t(q_ref[:, hs], lk_ref[:, hs]) * scale
        s = jnp.where(causal, s, -jnp.inf)
        e = jnp.exp(s - jnp.max(s, axis=1, keepdims=True))
        w = (e / jnp.sum(e, axis=1, keepdims=True)).astype(BF16)
        local = dot(w, lv_ref[:, hs])
        peak = st_ref[0, :, h : h + 1]
        for o in range(1, shards):
            peak = jnp.maximum(peak, st_ref[o, :, h : h + 1])
        num = jnp.zeros((rows, size), F32)
        den = jnp.zeros((rows, 1), F32)
        for o in range(shards):
            a = jnp.exp(st_ref[o, :, h : h + 1] - peak)
            num = num + a * n_ref[o, :, hs].astype(F32)
            den = den + a * st_ref[o, :, heads + h : heads + h + 1]
        gate = gate_ref[0:1, h : h + 1]
        mixed[:, hs] = ((gate / den) * num + (1.0 - gate) * local).astype(BF16)
    out_ref[...] = dot(mixed[...], ow_ref[...]).astype(BF16)


def body(queries, local_keys, local_values, memory_keys, memory_values, ids, gate_bias, out_weight):
    shards = lax.axis_size("mem")
    me = lax.axis_index("mem")
    rows, width = queries.shape
    heads = gate_bias.shape[0]
    size = width // heads
    memory_rows = memory_keys.shape[0]
    top = ids.shape[1]
    scale = size**-0.5
    background = top / (memory_rows * shards)
    group_ids = lax.all_gather(ids, "mem", axis=0, tiled=True) - me * memory_rows
    group_queries = lax.all_gather(queries, "mem", axis=0, tiled=True)
    weight = lax.all_gather(out_weight, "pb", axis=0, tiled=True)
    nums, stats = pl.pallas_call(
        functools.partial(shard_kernel, heads, scale, background),
        grid=(shards,),
        out_shape=(
            jax.ShapeDtypeStruct((shards * rows, width), BF16),
            jax.ShapeDtypeStruct((shards * rows, 128), F32),
        ),
        in_specs=[
            pl.BlockSpec((rows, top), lambda i: (i, 0)),
            pl.BlockSpec((rows, width), lambda i: (i, 0)),
            pl.BlockSpec((memory_rows, width), lambda i: (0, 0)),
            pl.BlockSpec((memory_rows, width), lambda i: (0, 0)),
        ],
        out_specs=(
            pl.BlockSpec((rows, width), lambda i: (i, 0)),
            pl.BlockSpec((rows, 128), lambda i: (i, 0)),
        ),
        scratch_shapes=[pltpu.VMEM((width, memory_rows), BF16)],
        compiler_params=pltpu.CompilerParams(vmem_limit_bytes=40 * 1024 * 1024),
        name="shard_attention",
    )(group_ids, group_queries, memory_keys, memory_values)
    nums = lax.all_to_all(nums, "mem", split_axis=0, concat_axis=0, tiled=True)
    stats = lax.all_to_all(stats[:, : 2 * heads], "mem", split_axis=0, concat_axis=0, tiled=True)
    gate = jax.nn.sigmoid(gate_bias)[None, :]
    return pl.pallas_call(
        functools.partial(final_kernel, heads, scale),
        out_shape=jax.ShapeDtypeStruct((rows, width), BF16),
        scratch_shapes=[pltpu.VMEM((rows, width), BF16)],
        compiler_params=pltpu.CompilerParams(vmem_limit_bytes=40 * 1024 * 1024),
        name="combine_and_project",
    )(
        queries,
        local_keys,
        local_values,
        nums.reshape(shards, rows, width),
        stats.reshape(shards, rows, 2 * heads),
        gate,
        weight,
    )


def solution(mesh):
    split = P(("pb", "mem"), None)
    in_specs = (split, split, split, P("mem", None), P("mem", None), split, P(), P("pb", None))
    return jax.shard_map(body, mesh=mesh, in_specs=in_specs, out_specs=split, check_vma=False)
```

```python
import functools

import jax
import jax.numpy as jnp
from jax import lax
from jax.experimental import pallas as pl
from jax.experimental.pallas import tpu as pltpu
from jax.sharding import PartitionSpec as P

LOG2E = 1.4426950408889634
F32 = jnp.float32
BF16 = jnp.bfloat16
MESH = pl.DeviceIdType.MESH
LANES = 128
ID_WIDTH = 256


def dot(a, b):
    return jnp.dot(a, b, preferred_element_type=F32)


def dot_t(a, b):
    return lax.dot_general(a, b, (((1,), (1,)), ((), ())), preferred_element_type=F32)


def copy_to(src, dst, send_sem, recv_sem, axis, index):
    return pltpu.make_async_remote_copy(
        src_ref=src,
        dst_ref=dst,
        send_sem=send_sem,
        recv_sem=recv_sem,
        device_id={axis: index},
        device_id_type=MESH,
    )


def count_block(ids, first_row, top, memory_rows, count_ref):
    lines = ids.shape[0]
    group = ID_WIDTH // top
    tiles = memory_rows // LANES
    local = ids - first_row
    high = jnp.right_shift(local, 7)
    low = jnp.bitwise_and(local, LANES - 1)
    place = lax.broadcasted_iota(jnp.int32, (tiles * group, ID_WIDTH), 0)
    entry = lax.broadcasted_iota(jnp.int32, (tiles * group, ID_WIDTH), 1)
    wanted = jnp.where(entry // top == place % group, place // group, -(2**30))
    lane = lax.broadcasted_iota(jnp.int32, (LANES, ID_WIDTH), 0)
    for line in range(lines):
        a = jnp.where(high[line : line + 1, :] == wanted, 1.0, 0.0).astype(BF16)
        b = jnp.where(low[line : line + 1, :] == lane, 1.0, 0.0).astype(BF16)
        c = dot_t(a, b)
        for tile in range(tiles):
            count_ref[line * group : (line + 1) * group, tile * LANES : (tile + 1) * LANES] = c[
                tile * group : (tile + 1) * group, :
            ]


def columns(parts, rows):
    used = sum(part.shape[0] for part in parts)
    if used < LANES:
        parts = parts + [jnp.zeros((LANES - used, rows), F32)]
    return jnp.concatenate(parts, axis=0).T


def kernel(
    shards,
    parts,
    heads,
    top,
    scale,
    background,
    q_ref,
    ids_ref,
    lk_ref,
    lv_ref,
    gate_ref,
    k_hbm,
    v_hbm,
    ow_hbm,
    out_ref,
    k_ref,
    kt_ref,
    v_ref,
    ow_ref,
    qbuf,
    idbuf,
    count_ref,
    nbuf,
    nst,
    rbuf,
    rst,
    cbuf,
    cst,
    fbuf,
    fst,
    local_ref,
    mixed,
    load_sem,
    q_send,
    q_recv,
    i_send,
    i_recv,
    r_send,
    r_recv,
    rs_send,
    rs_recv,
    f_send,
    f_recv,
    fs_send,
    fs_recv,
    ow_send,
    ow_recv,
):
    rows, width = q_ref.shape
    size = width // heads
    memory_rows = k_ref.shape[0]
    groups = shards // 2
    me = lax.axis_index("mem")
    mine = lax.axis_index("pb")
    column = lax.rem(me, 2)
    group = lax.div(me, 2)
    pair = me + 1 - 2 * column

    def peer(step):
        return lax.rem(group + step, groups) * 2 + column

    load_k = pltpu.make_async_copy(k_hbm, k_ref, load_sem.at[0])
    load_v = pltpu.make_async_copy(v_hbm, v_ref, load_sem.at[1])
    load_ow = pltpu.make_async_copy(ow_hbm, ow_ref.at[mine], load_sem.at[2])
    load_k.start()
    load_v.start()
    load_ow.start()
    qbuf[0] = q_ref[...]
    idbuf[0] = ids_ref[...]

    barrier = pltpu.get_barrier_semaphore()
    pl.semaphore_signal(barrier, inc=1, device_id={"mem": pair}, device_id_type=MESH)
    for step in range(1, groups):
        pl.semaphore_signal(barrier, inc=1, device_id={"mem": peer(step)}, device_id_type=MESH)
    for step in range(1, parts):
        pl.semaphore_signal(
            barrier, inc=1, device_id={"pb": lax.rem(mine + step, parts)}, device_id_type=MESH
        )
    pl.semaphore_wait(barrier, 1 + (groups - 1) + (parts - 1))

    def forward(j):
        return (
            copy_to(qbuf.at[2 * j], qbuf.at[2 * j + 1], q_send.at[j], q_recv.at[2 * j + 1], "mem", pair),
            copy_to(idbuf.at[2 * j], idbuf.at[2 * j + 1], i_send.at[j], i_recv.at[2 * j + 1], "mem", pair),
        )

    def spread(j):
        return (
            copy_to(qbuf.at[0], qbuf.at[2 * j], q_send.at[groups + j], q_recv.at[2 * j], "mem", peer(j)),
            copy_to(idbuf.at[0], idbuf.at[2 * j], i_send.at[groups + j], i_recv.at[2 * j], "mem", peer(j)),
        )

    def give(j):
        return (
            copy_to(nbuf.at[2 * j + 1], rbuf.at[j], r_send.at[j], r_recv.at[j], "mem", pair),
            copy_to(nst.at[2 * j + 1], rst.at[j], rs_send.at[j], rs_recv.at[j], "mem", pair),
        )

    def home(j):
        to = peer(groups - j)
        return (
            copy_to(cbuf.at[j], fbuf.at[j], f_send.at[j], f_recv.at[j], "mem", to),
            copy_to(cst.at[j], fst.at[j], fs_send.at[j], fs_recv.at[j], "mem", to),
        )

    def weight(step):
        return copy_to(
            ow_hbm,
            ow_ref.at[mine],
            ow_send.at[step],
            ow_recv.at[step],
            "pb",
            lax.rem(mine + step, parts),
        )

    for copy in forward(0):
        copy.start()
    for step in range(1, groups):
        for copy in spread(step):
            copy.start()
    for step in range(1, parts):
        weight(step).start()

    load_k.wait()
    for h in range(heads):
        hs = slice(h * size, (h + 1) * size)
        kt_ref[hs, :] = k_ref[:, hs].T

    causal = lax.broadcasted_iota(jnp.int32, (rows, rows), 0) >= lax.broadcasted_iota(
        jnp.int32, (rows, rows), 1
    )
    for h in range(heads):
        hs = slice(h * size, (h + 1) * size)
        s = dot_t(q_ref[:, hs], lk_ref[:, hs]) * scale
        s = jnp.where(causal, s, -jnp.inf)
        e = jnp.exp(s - jnp.max(s, axis=1, keepdims=True))
        w = (e / jnp.sum(e, axis=1, keepdims=True)).astype(BF16)
        local_ref[:, hs] = dot(w, lv_ref[:, hs]) * (1.0 - gate_ref[0:1, h : h + 1])
    load_v.wait()

    lane = lax.broadcasted_iota(jnp.int32, (rows, LANES), 1)

    def combine(j):
        for copy in give(j):
            copy.wait_recv()
        own_peak, own_den = nst[2 * j, :heads, :], nst[2 * j, heads:, :]
        got_peak, got_den = rst[j, :heads, :], rst[j, heads:, :]
        peak = jnp.maximum(own_peak, got_peak)
        own, got = jnp.exp(own_peak - peak), jnp.exp(got_peak - peak)
        cst[j, :heads, :] = peak
        cst[j, heads:, :] = own * own_den + got * got_den
        turned = columns([own, got], rows)
        for h in range(heads):
            hs = slice(h * size, (h + 1) * size)
            cbuf[j, :, hs] = (
                turned[:, h : h + 1] * nbuf[2 * j, :, hs].astype(F32)
                + turned[:, heads + h : heads + h + 1] * rbuf[j, :, hs].astype(F32)
            ).astype(BF16)

        @pl.when(j > 0)
        def _():
            for copy in home(j):
                copy.start()

    def step_of(i, carry):
        j = lax.div(i, 2)
        odd = lax.rem(i, 2)

        @pl.when(odd == 1)
        def _():
            for copy in forward(j):
                copy.wait_recv()

            @pl.when(j + 1 < groups)
            def _():
                for copy in spread(j + 1):
                    copy.wait_recv()
                for copy in forward(j + 1):
                    copy.start()

        count_block(idbuf[i], me * memory_rows, top, memory_rows, count_ref)
        stats = jnp.zeros((rows, LANES), F32)
        for h in range(heads):
            hs = slice(h * size, (h + 1) * size)
            s = dot(qbuf[i, :, hs], kt_ref[hs, :])
            peak = jnp.max(s, axis=1, keepdims=True)
            e = jnp.exp2((s - peak) * (scale * LOG2E))
            w = e * count_ref[...]
            total = jnp.sum(e, axis=1, keepdims=True)
            den = jnp.sum(w, axis=1, keepdims=True)
            nbuf[i, :, hs] = dot(w.astype(BF16), v_ref[:, hs]).astype(BF16)
            stats = jnp.where(lane == h, peak * scale, stats)
            stats = jnp.where(lane == heads + h, den + background * total, stats)
        nst[i] = stats.T[: 2 * heads, :]

        @pl.when(odd == 1)
        def _():
            for copy in give(j):
                copy.start()

            @pl.when(j > 0)
            def _():
                combine(j - 1)

        return carry

    lax.fori_loop(0, shards, step_of, 0)
    combine(groups - 1)

    for j in range(1, groups):
        for copy in home(j):
            copy.wait_recv()
    stats = [cst[0]] + [fst[j] for j in range(1, groups)]
    peak = stats[0][:heads, :]
    for st in stats[1:]:
        peak = jnp.maximum(peak, st[:heads, :])
    shares = [jnp.exp(st[:heads, :] - peak) for st in stats]
    den = shares[0] * stats[0][heads:, :]
    for share, st in zip(shares[1:], stats[1:]):
        den = den + share * st[heads:, :]
    turned = []
    per_turn = LANES // heads
    for first in range(0, groups, per_turn):
        turned.append(columns([share / den for share in shares[first : first + per_turn]], rows))
    for h in range(heads):
        hs = slice(h * size, (h + 1) * size)
        num = jnp.zeros((rows, size), F32)
        for j in range(groups):
            block = cbuf[0, :, hs] if j == 0 else fbuf[j, :, hs]
            at = (j % per_turn) * heads + h
            num = num + turned[j // per_turn][:, at : at + 1] * block.astype(F32)
        mixed[:, hs] = (gate_ref[0:1, h : h + 1] * num + local_ref[:, hs]).astype(BF16)

    load_ow.wait()
    for step in range(1, parts):
        weight(step).wait_recv()
    depth = width // parts
    result = dot(mixed[:, :depth], ow_ref[0])
    for part in range(1, parts):
        result = result + dot(mixed[:, part * depth : (part + 1) * depth], ow_ref[part])
    out_ref[...] = result.astype(BF16)

    for j in range(groups):
        for copy in forward(j) + give(j):
            copy.wait_send()
    for j in range(1, groups):
        for copy in spread(j) + home(j):
            copy.wait_send()
    for step in range(1, parts):
        weight(step).wait_send()


def body(queries, local_keys, local_values, memory_keys, memory_values, ids, gate_bias, out_weight):
    shards = lax.axis_size("mem")
    parts = lax.axis_size("pb")
    rows, width = queries.shape
    heads = gate_bias.shape[0]
    memory_rows = memory_keys.shape[0]
    top = ids.shape[1]
    groups = shards // 2
    lines = rows * top // ID_WIDTH
    gate = jax.nn.sigmoid(gate_bias)[None, :]
    vmem = pl.BlockSpec(memory_space=pltpu.VMEM)
    hbm = pl.BlockSpec(memory_space=pl.ANY)
    dma = pltpu.SemaphoreType.DMA
    return pl.pallas_call(
        functools.partial(
            kernel,
            shards,
            parts,
            heads,
            top,
            (width // heads) ** -0.5,
            top / (memory_rows * shards),
        ),
        out_shape=jax.ShapeDtypeStruct((rows, width), BF16),
        in_specs=[vmem] * 5 + [hbm] * 3,
        out_specs=vmem,
        scratch_shapes=[
            pltpu.VMEM((memory_rows, width), BF16),
            pltpu.VMEM((width, memory_rows), BF16),
            pltpu.VMEM((memory_rows, width), BF16),
            pltpu.VMEM((parts, width // parts, width), BF16),
            pltpu.VMEM((shards, rows, width), BF16),
            pltpu.VMEM((shards, lines, ID_WIDTH), jnp.int32),
            pltpu.VMEM((rows, memory_rows), F32),
            pltpu.VMEM((shards, rows, width), BF16),
            pltpu.VMEM((shards, 2 * heads, rows), F32),
            pltpu.VMEM((groups, rows, width), BF16),
            pltpu.VMEM((groups, 2 * heads, rows), F32),
            pltpu.VMEM((groups, rows, width), BF16),
            pltpu.VMEM((groups, 2 * heads, rows), F32),
            pltpu.VMEM((groups, rows, width), BF16),
            pltpu.VMEM((groups, 2 * heads, rows), F32),
            pltpu.VMEM((rows, width), F32),
            pltpu.VMEM((rows, width), BF16),
            dma((3,)),
            dma((shards,)),
            dma((shards,)),
            dma((shards,)),
            dma((shards,)),
            dma((groups,)),
            dma((groups,)),
            dma((groups,)),
            dma((groups,)),
            dma((groups,)),
            dma((groups,)),
            dma((groups,)),
            dma((groups,)),
            dma((parts,)),
            dma((parts,)),
        ],
        compiler_params=pltpu.CompilerParams(
            collective_id=0, has_side_effects=True, vmem_limit_bytes=56 * 1024 * 1024
        ),
        name="retrieval_attention",
    )(
        queries,
        ids.reshape(lines, ID_WIDTH),
        local_keys,
        local_values,
        gate,
        memory_keys,
        memory_values,
        out_weight,
    )


def solution(mesh):
    split = P(("pb", "mem"), None)
    in_specs = (split, split, split, P("mem", None), P("mem", None), split, P(), P("pb", None))
    return jax.shard_map(body, mesh=mesh, in_specs=in_specs, out_specs=split, check_vma=False)
```

```python
import functools

import jax
import jax.numpy as jnp
from jax import lax
from jax.experimental import pallas as pl
from jax.experimental.pallas import tpu as pltpu
from jax.sharding import PartitionSpec as P

LOG2E = 1.4426950408889634
F32 = jnp.float32
BF16 = jnp.bfloat16
MESH = pl.DeviceIdType.MESH
LANES = 128
ID_WIDTH = 256


def dot(a, b):
    return jnp.dot(a, b, preferred_element_type=F32)


def dot_t(a, b):
    return lax.dot_general(a, b, (((1,), (1,)), ((), ())), preferred_element_type=F32)


def copy_to(src, dst, send_sem, recv_sem, axis, index):
    return pltpu.make_async_remote_copy(
        src_ref=src,
        dst_ref=dst,
        send_sem=send_sem,
        recv_sem=recv_sem,
        device_id={axis: index},
        device_id_type=MESH,
    )


def count_block(ids, first_row, top, memory_rows, count_ref):
    lines = ids.shape[0]
    group = ID_WIDTH // top
    tiles = memory_rows // LANES
    local = ids - first_row
    high = jnp.right_shift(local, 7)
    low = jnp.bitwise_and(local, LANES - 1)
    place = lax.broadcasted_iota(jnp.int32, (tiles * group, ID_WIDTH), 0)
    entry = lax.broadcasted_iota(jnp.int32, (tiles * group, ID_WIDTH), 1)
    wanted = jnp.where(entry // top == place % group, place // group, -(2**30))
    lane = lax.broadcasted_iota(jnp.int32, (LANES, ID_WIDTH), 0)
    for line in range(lines):
        a = jnp.where(high[line : line + 1, :] == wanted, 1.0, 0.0).astype(BF16)
        b = jnp.where(low[line : line + 1, :] == lane, 1.0, 0.0).astype(BF16)
        c = dot_t(a, b)
        for tile in range(tiles):
            count_ref[line * group : (line + 1) * group, tile * LANES : (tile + 1) * LANES] = c[
                tile * group : (tile + 1) * group, :
            ]


def columns(parts, rows):
    used = sum(part.shape[0] for part in parts)
    if used < LANES:
        parts = parts + [jnp.zeros((LANES - used, rows), F32)]
    return jnp.concatenate(parts, axis=0).T


def kernel(
    shards,
    parts,
    heads,
    top,
    scale,
    background,
    q_ref,
    ids_ref,
    lk_ref,
    lv_ref,
    gate_ref,
    k_hbm,
    v_hbm,
    ow_hbm,
    out_ref,
    k_ref,
    kt_ref,
    v_ref,
    ow_ref,
    qbuf,
    idbuf,
    count_ref,
    nbuf,
    nst,
    rbuf,
    rst,
    cbuf,
    cst,
    fbuf,
    fst,
    local_ref,
    mixed,
    load_sem,
    q_send,
    q_recv,
    i_send,
    i_recv,
    r_send,
    r_recv,
    rs_send,
    rs_recv,
    f_send,
    f_recv,
    fs_send,
    fs_recv,
    ow_send,
    ow_recv,
):
    rows, width = q_ref.shape
    size = width // heads
    memory_rows = k_ref.shape[0]
    groups = shards // 2
    me = lax.axis_index("mem")
    mine = lax.axis_index("pb")
    column = lax.rem(me, 2)
    group = lax.div(me, 2)
    pair = me + 1 - 2 * column

    def peer(step):
        return lax.rem(group + step, groups) * 2 + column

    def away(j):
        up = j % 2
        return up * ((j + 1) // 2) + (1 - up) * (groups - j // 2)

    load_k = pltpu.make_async_copy(k_hbm, k_ref, load_sem.at[0])
    load_v = pltpu.make_async_copy(v_hbm, v_ref, load_sem.at[1])
    load_ow = pltpu.make_async_copy(ow_hbm, ow_ref.at[mine], load_sem.at[2])
    load_k.start()
    load_v.start()
    load_ow.start()
    qbuf[0] = q_ref[...]
    idbuf[0] = ids_ref[...]

    barrier = pltpu.get_barrier_semaphore()
    pl.semaphore_signal(barrier, inc=1, device_id={"mem": pair}, device_id_type=MESH)
    for step in range(1, groups):
        pl.semaphore_signal(barrier, inc=1, device_id={"mem": peer(step)}, device_id_type=MESH)
    for step in range(1, parts):
        pl.semaphore_signal(
            barrier, inc=1, device_id={"pb": lax.rem(mine + step, parts)}, device_id_type=MESH
        )
    pl.semaphore_wait(barrier, 1 + (groups - 1) + (parts - 1))

    def forward(j):
        return (
            copy_to(qbuf.at[2 * j], qbuf.at[2 * j + 1], q_send.at[j], q_recv.at[2 * j + 1], "mem", pair),
            copy_to(idbuf.at[2 * j], idbuf.at[2 * j + 1], i_send.at[j], i_recv.at[2 * j + 1], "mem", pair),
        )

    def spread(j):
        return (
            copy_to(qbuf.at[0], qbuf.at[2 * j], q_send.at[groups + j], q_recv.at[2 * j], "mem", peer(away(j))),
            copy_to(idbuf.at[0], idbuf.at[2 * j], i_send.at[groups + j], i_recv.at[2 * j], "mem", peer(away(j))),
        )

    def give(j):
        return (
            copy_to(nbuf.at[2 * j + 1], rbuf.at[j], r_send.at[j], r_recv.at[j], "mem", pair),
            copy_to(nst.at[2 * j + 1], rst.at[j], rs_send.at[j], rs_recv.at[j], "mem", pair),
        )

    def home(j):
        to = peer(groups - away(j))
        return (
            copy_to(cbuf.at[j], fbuf.at[j], f_send.at[j], f_recv.at[j], "mem", to),
            copy_to(cst.at[j], fst.at[j], fs_send.at[j], fs_recv.at[j], "mem", to),
        )

    def weight(step):
        return copy_to(
            ow_hbm,
            ow_ref.at[mine],
            ow_send.at[step],
            ow_recv.at[step],
            "pb",
            lax.rem(mine + step, parts),
        )

    for copy in forward(0):
        copy.start()
    for step in range(1, min(3, groups)):
        for copy in spread(step):
            copy.start()
    for step in range(1, parts):
        weight(step).start()

    load_k.wait()
    for h in range(heads):
        hs = slice(h * size, (h + 1) * size)
        kt_ref[hs, :] = k_ref[:, hs].T

    causal = lax.broadcasted_iota(jnp.int32, (rows, rows), 0) >= lax.broadcasted_iota(
        jnp.int32, (rows, rows), 1
    )
    for h in range(heads):
        hs = slice(h * size, (h + 1) * size)
        s = dot_t(q_ref[:, hs], lk_ref[:, hs]) * scale
        s = jnp.where(causal, s, -jnp.inf)
        e = jnp.exp(s - jnp.max(s, axis=1, keepdims=True))
        w = (e / jnp.sum(e, axis=1, keepdims=True)).astype(BF16)
        local_ref[:, hs] = dot(w, lv_ref[:, hs]) * (1.0 - gate_ref[0:1, h : h + 1])
    load_v.wait()
    for step in range(3, groups):
        for copy in spread(step):
            copy.start()

    lane = lax.broadcasted_iota(jnp.int32, (rows, LANES), 1)

    def combine(j):
        for copy in give(j):
            copy.wait_recv()
        own_peak, own_den = nst[2 * j, :heads, :], nst[2 * j, heads:, :]
        got_peak, got_den = rst[j, :heads, :], rst[j, heads:, :]
        peak = jnp.maximum(own_peak, got_peak)
        own, got = jnp.exp(own_peak - peak), jnp.exp(got_peak - peak)
        cst[j, :heads, :] = peak
        cst[j, heads:, :] = own * own_den + got * got_den
        turned = columns([own, got], rows)
        for h in range(heads):
            hs = slice(h * size, (h + 1) * size)
            cbuf[j, :, hs] = (
                turned[:, h : h + 1] * nbuf[2 * j, :, hs].astype(F32)
                + turned[:, heads + h : heads + h + 1] * rbuf[j, :, hs].astype(F32)
            ).astype(BF16)

        @pl.when(j > 0)
        def _():
            for copy in home(j):
                copy.start()

    def step_of(i, carry):
        j = lax.div(i, 2)
        odd = lax.rem(i, 2)

        @pl.when((odd == 0) & (j + 1 < groups))
        def _():
            for copy in spread(j + 1):
                copy.wait_recv()
            for copy in forward(j + 1):
                copy.start()

        @pl.when(odd == 1)
        def _():
            for copy in forward(j):
                copy.wait_recv()

        count_block(idbuf[i], me * memory_rows, top, memory_rows, count_ref)
        stats = jnp.zeros((rows, LANES), F32)
        for h in range(heads):
            hs = slice(h * size, (h + 1) * size)
            s = dot(qbuf[i, :, hs], kt_ref[hs, :])
            peak = jnp.max(s, axis=1, keepdims=True)
            e = jnp.exp2((s - peak) * (scale * LOG2E))
            w = e * count_ref[...]
            total = jnp.sum(e, axis=1, keepdims=True)
            den = jnp.sum(w, axis=1, keepdims=True)
            nbuf[i, :, hs] = dot(w.astype(BF16), v_ref[:, hs]).astype(BF16)
            stats = jnp.where(lane == h, peak * scale, stats)
            stats = jnp.where(lane == heads + h, den + background * total, stats)
        nst[i] = stats.T[: 2 * heads, :]

        @pl.when(odd == 1)
        def _():
            for copy in give(j):
                copy.start()

            @pl.when(j > 0)
            def _():
                combine(j - 1)

        return carry

    lax.fori_loop(0, shards, step_of, 0)
    combine(groups - 1)

    for j in range(1, groups):
        for copy in home(j):
            copy.wait_recv()
    stats = [cst[0]] + [fst[j] for j in range(1, groups)]
    peak = stats[0][:heads, :]
    for st in stats[1:]:
        peak = jnp.maximum(peak, st[:heads, :])
    shares = [jnp.exp(st[:heads, :] - peak) for st in stats]
    den = shares[0] * stats[0][heads:, :]
    for share, st in zip(shares[1:], stats[1:]):
        den = den + share * st[heads:, :]
    turned = []
    per_turn = LANES // heads
    for first in range(0, groups, per_turn):
        turned.append(columns([share / den for share in shares[first : first + per_turn]], rows))
    for h in range(heads):
        hs = slice(h * size, (h + 1) * size)
        num = jnp.zeros((rows, size), F32)
        for j in range(groups):
            block = cbuf[0, :, hs] if j == 0 else fbuf[j, :, hs]
            at = (j % per_turn) * heads + h
            num = num + turned[j // per_turn][:, at : at + 1] * block.astype(F32)
        mixed[:, hs] = (gate_ref[0:1, h : h + 1] * num + local_ref[:, hs]).astype(BF16)

    load_ow.wait()
    for step in range(1, parts):
        weight(step).wait_recv()
    depth = width // parts
    result = dot(mixed[:, :depth], ow_ref[0])
    for part in range(1, parts):
        result = result + dot(mixed[:, part * depth : (part + 1) * depth], ow_ref[part])
    out_ref[...] = result.astype(BF16)

    for j in range(groups):
        for copy in forward(j) + give(j):
            copy.wait_send()
    for j in range(1, groups):
        for copy in spread(j) + home(j):
            copy.wait_send()
    for step in range(1, parts):
        weight(step).wait_send()


def body(queries, local_keys, local_values, memory_keys, memory_values, ids, gate_bias, out_weight):
    shards = lax.axis_size("mem")
    parts = lax.axis_size("pb")
    rows, width = queries.shape
    heads = gate_bias.shape[0]
    memory_rows = memory_keys.shape[0]
    top = ids.shape[1]
    groups = shards // 2
    lines = rows * top // ID_WIDTH
    gate = jax.nn.sigmoid(gate_bias)[None, :]
    vmem = pl.BlockSpec(memory_space=pltpu.VMEM)
    hbm = pl.BlockSpec(memory_space=pl.ANY)
    dma = pltpu.SemaphoreType.DMA
    return pl.pallas_call(
        functools.partial(
            kernel,
            shards,
            parts,
            heads,
            top,
            (width // heads) ** -0.5,
            top / (memory_rows * shards),
        ),
        out_shape=jax.ShapeDtypeStruct((rows, width), BF16),
        in_specs=[vmem] * 5 + [hbm] * 3,
        out_specs=vmem,
        scratch_shapes=[
            pltpu.VMEM((memory_rows, width), BF16),
            pltpu.VMEM((width, memory_rows), BF16),
            pltpu.VMEM((memory_rows, width), BF16),
            pltpu.VMEM((parts, width // parts, width), BF16),
            pltpu.VMEM((shards, rows, width), BF16),
            pltpu.VMEM((shards, lines, ID_WIDTH), jnp.int32),
            pltpu.VMEM((rows, memory_rows), F32),
            pltpu.VMEM((shards, rows, width), BF16),
            pltpu.VMEM((shards, 2 * heads, rows), F32),
            pltpu.VMEM((groups, rows, width), BF16),
            pltpu.VMEM((groups, 2 * heads, rows), F32),
            pltpu.VMEM((groups, rows, width), BF16),
            pltpu.VMEM((groups, 2 * heads, rows), F32),
            pltpu.VMEM((groups, rows, width), BF16),
            pltpu.VMEM((groups, 2 * heads, rows), F32),
            pltpu.VMEM((rows, width), F32),
            pltpu.VMEM((rows, width), BF16),
            dma((3,)),
            dma((shards,)),
            dma((shards,)),
            dma((shards,)),
            dma((shards,)),
            dma((groups,)),
            dma((groups,)),
            dma((groups,)),
            dma((groups,)),
            dma((groups,)),
            dma((groups,)),
            dma((groups,)),
            dma((groups,)),
            dma((parts,)),
            dma((parts,)),
        ],
        compiler_params=pltpu.CompilerParams(
            collective_id=0, has_side_effects=True, vmem_limit_bytes=56 * 1024 * 1024
        ),
        name="retrieval_attention",
    )(
        queries,
        ids.reshape(lines, ID_WIDTH),
        local_keys,
        local_values,
        gate,
        memory_keys,
        memory_values,
        out_weight,
    )


def solution(mesh):
    split = P(("pb", "mem"), None)
    in_specs = (split, split, split, P("mem", None), P("mem", None), split, P(), P("pb", None))
    return jax.shard_map(body, mesh=mesh, in_specs=in_specs, out_specs=split, check_vma=False)
```

```python
import functools

import jax
import jax.numpy as jnp
from jax import lax
from jax.experimental import pallas as pl
from jax.experimental.pallas import tpu as pltpu
from jax.sharding import PartitionSpec as P

LOG2E = 1.4426950408889634
F32 = jnp.float32
BF16 = jnp.bfloat16
MESH = pl.DeviceIdType.MESH
LANES = 128
ID_WIDTH = 256


def dot(a, b):
    return jnp.dot(a, b, preferred_element_type=F32)


def dot_t(a, b):
    return lax.dot_general(a, b, (((1,), (1,)), ((), ())), preferred_element_type=F32)


def copy_to(src, dst, send_sem, recv_sem, axis, index):
    return pltpu.make_async_remote_copy(
        src_ref=src,
        dst_ref=dst,
        send_sem=send_sem,
        recv_sem=recv_sem,
        device_id={axis: index},
        device_id_type=MESH,
    )


def count_block(ids, first_row, top, memory_rows, count_ref):
    lines = ids.shape[0]
    group = ID_WIDTH // top
    tiles = memory_rows // LANES
    local = ids - first_row
    high = jnp.right_shift(local, 7)
    low = jnp.bitwise_and(local, LANES - 1)
    place = lax.broadcasted_iota(jnp.int32, (tiles * group, ID_WIDTH), 0)
    entry = lax.broadcasted_iota(jnp.int32, (tiles * group, ID_WIDTH), 1)
    wanted = jnp.where(entry // top == place % group, place // group, -(2**30))
    lane = lax.broadcasted_iota(jnp.int32, (LANES, ID_WIDTH), 0)
    for line in range(lines):
        a = jnp.where(high[line : line + 1, :] == wanted, 1.0, 0.0).astype(BF16)
        b = jnp.where(low[line : line + 1, :] == lane, 1.0, 0.0).astype(BF16)
        c = dot_t(a, b)
        for tile in range(tiles):
            count_ref[line * group : (line + 1) * group, tile * LANES : (tile + 1) * LANES] = c[
                tile * group : (tile + 1) * group, :
            ]


def columns(parts, rows):
    used = sum(part.shape[0] for part in parts)
    if used < LANES:
        parts = parts + [jnp.zeros((LANES - used, rows), F32)]
    return jnp.concatenate(parts, axis=0).T


def kernel(
    shards,
    parts,
    heads,
    top,
    scale,
    background,
    q_ref,
    ids_ref,
    lk_ref,
    lv_ref,
    gate_ref,
    k_hbm,
    v_hbm,
    ow_hbm,
    out_ref,
    k_ref,
    kt_ref,
    v_ref,
    ow_ref,
    qbuf,
    idbuf,
    count_ref,
    nbuf,
    nst,
    rbuf,
    rst,
    cbuf,
    cst,
    fbuf,
    fst,
    local_ref,
    mixed,
    load_sem,
    q_send,
    q_recv,
    i_send,
    i_recv,
    r_send,
    r_recv,
    rs_send,
    rs_recv,
    f_send,
    f_recv,
    fs_send,
    fs_recv,
    ow_send,
    ow_recv,
):
    rows, width = q_ref.shape
    size = width // heads
    memory_rows = k_ref.shape[0]
    groups = shards // 2
    me = lax.axis_index("mem")
    mine = lax.axis_index("pb")
    column = lax.rem(me, 2)
    group = lax.div(me, 2)
    pair = me + 1 - 2 * column

    def peer(step):
        return lax.rem(group + step, groups) * 2 + column

    load_k = pltpu.make_async_copy(k_hbm, k_ref, load_sem.at[0])
    load_v = pltpu.make_async_copy(v_hbm, v_ref, load_sem.at[1])
    load_ow = pltpu.make_async_copy(ow_hbm, ow_ref.at[mine], load_sem.at[2])
    load_k.start()
    load_v.start()
    load_ow.start()
    qbuf[0] = q_ref[...]
    idbuf[0] = ids_ref[...]

    barrier = pltpu.get_barrier_semaphore()
    pl.semaphore_signal(barrier, inc=1, device_id={"mem": pair}, device_id_type=MESH)
    for step in range(1, groups):
        pl.semaphore_signal(barrier, inc=1, device_id={"mem": peer(step)}, device_id_type=MESH)
    for step in range(1, parts):
        pl.semaphore_signal(
            barrier, inc=1, device_id={"pb": lax.rem(mine + step, parts)}, device_id_type=MESH
        )
    pl.semaphore_wait(barrier, 1 + (groups - 1) + (parts - 1))

    def forward(j):
        return (
            copy_to(qbuf.at[2 * j], qbuf.at[2 * j + 1], q_send.at[j], q_recv.at[2 * j + 1], "mem", pair),
            copy_to(idbuf.at[2 * j], idbuf.at[2 * j + 1], i_send.at[j], i_recv.at[2 * j + 1], "mem", pair),
        )

    def spread(j):
        return (
            copy_to(qbuf.at[0], qbuf.at[2 * j], q_send.at[groups + j], q_recv.at[2 * j], "mem", peer(j)),
            copy_to(idbuf.at[0], idbuf.at[2 * j], i_send.at[groups + j], i_recv.at[2 * j], "mem", peer(j)),
        )

    def give(j):
        return (
            copy_to(nbuf.at[2 * j + 1], rbuf.at[j], r_send.at[j], r_recv.at[j], "mem", pair),
            copy_to(nst.at[2 * j + 1], rst.at[j], rs_send.at[j], rs_recv.at[j], "mem", pair),
        )

    def home(j):
        to = peer(groups - j)
        return (
            copy_to(cbuf.at[j], fbuf.at[j], f_send.at[j], f_recv.at[j], "mem", to),
            copy_to(cst.at[j], fst.at[j], fs_send.at[j], fs_recv.at[j], "mem", to),
        )

    def weight(step):
        return copy_to(
            ow_hbm,
            ow_ref.at[mine],
            ow_send.at[step],
            ow_recv.at[step],
            "pb",
            lax.rem(mine + step, parts),
        )

    for copy in forward(0):
        copy.start()
    for step in range(1, groups):
        for copy in spread(step):
            copy.start()
    for step in range(1, parts):
        weight(step).start()

    load_k.wait()
    gate = 1.0 / (1.0 + jnp.exp(-gate_ref[...]))
    for h in range(heads):
        hs = slice(h * size, (h + 1) * size)
        kt_ref[hs, :] = k_ref[:, hs].T

    causal = lax.broadcasted_iota(jnp.int32, (rows, rows), 0) >= lax.broadcasted_iota(
        jnp.int32, (rows, rows), 1
    )
    for h in range(heads):
        hs = slice(h * size, (h + 1) * size)
        s = dot_t(q_ref[:, hs], lk_ref[:, hs]) * scale
        s = jnp.where(causal, s, -jnp.inf)
        e = jnp.exp(s - jnp.max(s, axis=1, keepdims=True))
        w = (e / jnp.sum(e, axis=1, keepdims=True)).astype(BF16)
        local_ref[:, hs] = dot(w, lv_ref[:, hs]) * (1.0 - gate[0:1, h : h + 1])
    load_v.wait()

    lane = lax.broadcasted_iota(jnp.int32, (rows, LANES), 1)

    def combine(j):
        for copy in give(j):
            copy.wait_recv()
        own_peak, own_den = nst[2 * j, :heads, :], nst[2 * j, heads:, :]
        got_peak, got_den = rst[j, :heads, :], rst[j, heads:, :]
        peak = jnp.maximum(own_peak, got_peak)
        own, got = jnp.exp(own_peak - peak), jnp.exp(got_peak - peak)
        cst[j, :heads, :] = peak
        cst[j, heads:, :] = own * own_den + got * got_den
        turned = columns([own, got], rows)
        for h in range(heads):
            hs = slice(h * size, (h + 1) * size)
            cbuf[j, :, hs] = (
                turned[:, h : h + 1] * nbuf[2 * j, :, hs].astype(F32)
                + turned[:, heads + h : heads + h + 1] * rbuf[j, :, hs].astype(F32)
            ).astype(BF16)

        @pl.when(j > 0)
        def _():
            for copy in home(j):
                copy.start()

    def step_of(i, carry):
        j = lax.div(i, 2)
        odd = lax.rem(i, 2)

        @pl.when(odd == 1)
        def _():
            for copy in forward(j):
                copy.wait_recv()

            @pl.when(j + 1 < groups)
            def _():
                for copy in spread(j + 1):
                    copy.wait_recv()
                for copy in forward(j + 1):
                    copy.start()

        count_block(idbuf[i], me * memory_rows, top, memory_rows, count_ref)
        stats = jnp.zeros((rows, LANES), F32)
        for h in range(heads):
            hs = slice(h * size, (h + 1) * size)
            s = dot(qbuf[i, :, hs], kt_ref[hs, :])
            peak = jnp.max(s, axis=1, keepdims=True)
            e = jnp.exp2((s - peak) * (scale * LOG2E))
            w = e * count_ref[...]
            total = jnp.sum(e, axis=1, keepdims=True)
            den = jnp.sum(w, axis=1, keepdims=True)
            nbuf[i, :, hs] = dot(w.astype(BF16), v_ref[:, hs]).astype(BF16)
            stats = jnp.where(lane == h, peak * scale, stats)
            stats = jnp.where(lane == heads + h, den + background * total, stats)
        nst[i] = stats.T[: 2 * heads, :]

        @pl.when(odd == 1)
        def _():
            for copy in give(j):
                copy.start()

            @pl.when(j > 0)
            def _():
                combine(j - 1)

        return carry

    lax.fori_loop(0, shards, step_of, 0)
    combine(groups - 1)

    for j in range(1, groups):
        for copy in home(j):
            copy.wait_recv()
    stats = [cst[0]] + [fst[j] for j in range(1, groups)]
    peak = stats[0][:heads, :]
    for st in stats[1:]:
        peak = jnp.maximum(peak, st[:heads, :])
    shares = [jnp.exp(st[:heads, :] - peak) for st in stats]
    den = shares[0] * stats[0][heads:, :]
    for share, st in zip(shares[1:], stats[1:]):
        den = den + share * st[heads:, :]
    turned = []
    per_turn = LANES // heads
    for first in range(0, groups, per_turn):
        turned.append(columns([share / den for share in shares[first : first + per_turn]], rows))
    for h in range(heads):
        hs = slice(h * size, (h + 1) * size)
        num = jnp.zeros((rows, size), F32)
        for j in range(groups):
            block = cbuf[0, :, hs] if j == 0 else fbuf[j, :, hs]
            at = (j % per_turn) * heads + h
            num = num + turned[j // per_turn][:, at : at + 1] * block.astype(F32)
        mixed[:, hs] = (gate[0:1, h : h + 1] * num + local_ref[:, hs]).astype(BF16)

    load_ow.wait()
    for step in range(1, parts):
        weight(step).wait_recv()
    depth = width // parts
    result = dot(mixed[:, :depth], ow_ref[0])
    for part in range(1, parts):
        result = result + dot(mixed[:, part * depth : (part + 1) * depth], ow_ref[part])
    out_ref[...] = result.astype(BF16)

    for j in range(groups):
        for copy in forward(j) + give(j):
            copy.wait_send()
    for j in range(1, groups):
        for copy in spread(j) + home(j):
            copy.wait_send()
    for step in range(1, parts):
        weight(step).wait_send()


def body(queries, local_keys, local_values, memory_keys, memory_values, ids, gate_bias, out_weight):
    shards = lax.axis_size("mem")
    parts = lax.axis_size("pb")
    rows, width = queries.shape
    heads = gate_bias.shape[0]
    memory_rows = memory_keys.shape[0]
    top = ids.shape[1]
    groups = shards // 2
    lines = rows * top // ID_WIDTH
    vmem = pl.BlockSpec(memory_space=pltpu.VMEM)
    hbm = pl.BlockSpec(memory_space=pl.ANY)
    dma = pltpu.SemaphoreType.DMA
    return pl.pallas_call(
        functools.partial(
            kernel,
            shards,
            parts,
            heads,
            top,
            (width // heads) ** -0.5,
            top / (memory_rows * shards),
        ),
        out_shape=jax.ShapeDtypeStruct((rows, width), BF16),
        in_specs=[vmem] * 5 + [hbm] * 3,
        out_specs=vmem,
        scratch_shapes=[
            pltpu.VMEM((memory_rows, width), BF16),
            pltpu.VMEM((width, memory_rows), BF16),
            pltpu.VMEM((memory_rows, width), BF16),
            pltpu.VMEM((parts, width // parts, width), BF16),
            pltpu.VMEM((shards, rows, width), BF16),
            pltpu.VMEM((shards, lines, ID_WIDTH), jnp.int32),
            pltpu.VMEM((rows, memory_rows), F32),
            pltpu.VMEM((shards, rows, width), BF16),
            pltpu.VMEM((shards, 2 * heads, rows), F32),
            pltpu.VMEM((groups, rows, width), BF16),
            pltpu.VMEM((groups, 2 * heads, rows), F32),
            pltpu.VMEM((groups, rows, width), BF16),
            pltpu.VMEM((groups, 2 * heads, rows), F32),
            pltpu.VMEM((groups, rows, width), BF16),
            pltpu.VMEM((groups, 2 * heads, rows), F32),
            pltpu.VMEM((rows, width), F32),
            pltpu.VMEM((rows, width), BF16),
            dma((3,)),
            dma((shards,)),
            dma((shards,)),
            dma((shards,)),
            dma((shards,)),
            dma((groups,)),
            dma((groups,)),
            dma((groups,)),
            dma((groups,)),
            dma((groups,)),
            dma((groups,)),
            dma((groups,)),
            dma((groups,)),
            dma((parts,)),
            dma((parts,)),
        ],
        compiler_params=pltpu.CompilerParams(
            collective_id=0, has_side_effects=True, vmem_limit_bytes=56 * 1024 * 1024
        ),
        name="retrieval_attention",
    )(
        queries,
        ids.reshape(lines, ID_WIDTH),
        local_keys,
        local_values,
        gate_bias[None, :],
        memory_keys,
        memory_values,
        out_weight,
    )


def solution(mesh):
    split = P(("pb", "mem"), None)
    in_specs = (split, split, split, P("mem", None), P("mem", None), split, P(), P("pb", None))
    return jax.shard_map(body, mesh=mesh, in_specs=in_specs, out_specs=split, check_vma=False)
```
